128 devices in a mesh: replica: 8 (over x_hi, z), zero: 16 (over x_lo, y, core).
Axes of the slice: x: 4 (x_hi: 2, x_lo: 2; x = x_hi * 2 + x_lo), y: 4, z: 4, core: 2. Of those that a mesh axis runs over, the one named last changes fastest.
Arguments:
- grads_pair: bfloat16 [128, 2, 64, 28672], P(('replica', 'zero')), may hold values from -24 to 24
- grads_down: bfloat16 [128, 128, 8192], P(('replica', 'zero')), may hold values from -24 to 24
- inner_pair: float32 [8, 2, 64, 28672], P('replica', None, None, 'zero'), may hold values from -6 to 6
- inner_down: float32 [8, 128, 8192], P('replica', None, 'zero'), may hold values from -6 to 6
- first_pair: float32 [8, 2, 64, 28672], P('replica', None, None, 'zero'), may hold values from -2.4 to 2.4
- first_down: float32 [8, 128, 8192], P('replica', None, 'zero'), may hold values from -2.4 to 2.4
- second_pair: float32 [8, 2, 64, 28672], P('replica', None, None, 'zero'), may hold values from 0.1 to 2
- second_down: float32 [8, 128, 8192], P('replica', None, 'zero'), may hold values from 0.1 to 2
- anchor_pair: float32 [2, 64, 28672], P(None, None, 'zero'), may hold values from -6 to 6
- anchor_down: float32 [128, 8192], P(None, 'zero'), may hold values from -6 to 6
- velocity_pair: float32 [2, 64, 28672], P(None, None, 'zero'), may hold values from -1.8 to 1.8
- velocity_down: float32 [128, 8192], P(None, 'zero'), may hold values from -1.8 to 1.8
Outputs:
- weights_pair: bfloat16 [2, 64, 28672], replicated
- weights_down: bfloat16 [128, 8192], replicated
- anchor_pair_next: float32 [2, 64, 28672], P(None, 'replica', 'zero')
- anchor_down_next: float32 [128, 8192], P('replica', 'zero')
- velocity_pair_next: float32 [2, 64, 28672], P(None, 'replica', 'zero')
- velocity_down_next: float32 [128, 8192], P('replica', 'zero')
The draws below stay inside these ranges and needn't reach their ends.
All inputs are finite; a program needn't handle non-finite values.
Results may differ from the reference program's by a relative error of at most 0.00185.
Values may be sent and summed in bfloat16 or wider, within the bound.
A program may use at most 128 MiB of HBM per device.

```python
import math
import jax
import jax.numpy as jnp
from jax import lax

D = 8192
FF = 28672
ROWS = 64
DROWS = 128
INNER_STEP = 500
WORKERS = 128
N_REPLICA = 8
N_ZERO = 16


def raised(values, key, source, target, shards_of, factor):
    def block_of(axis_at):
        return (jnp.arange(values.shape[axis_at]) // (values.shape[axis_at] // shards_of)).reshape((-1,) + (1,) * (values.ndim - 1 - axis_at))

    one_side = jax.random.permutation(key, shards_of)[block_of(target)]
    far = (block_of(target) + shards_of // 2) % shards_of
    return jnp.where((block_of(source) == one_side) | (block_of(source) == far), factor * values, values)


def steps_of(key, dims, cuts, least, high):
    level, own = 1.0, jax.random.fold_in(key, 6)
    for dim, shards_of in cuts:
        heights = jnp.exp(jax.random.uniform(jax.random.fold_in(own, dim), (shards_of,), jnp.float32, least / len(cuts), high / len(cuts)))
        level = level * jnp.repeat(heights, dims[dim] // shards_of).reshape([-1 if axis == dim else 1 for axis in range(len(dims))])
    return level


def gaussian(key, shape, deviation, bound, shards=(), dtype=jnp.bfloat16):
    entries = deviation * jax.random.normal(key, shape, jnp.float32)
    if shards:
        entries = entries * steps_of(key, shape, shards, -0.22, 0.18)
    return jnp.clip(entries, -bound, bound).astype(dtype)


def heavy_noise(key, shape, scale, most, shards, heavy, dtype=jnp.bfloat16):
    values = scale * jax.random.normal(key, shape, jnp.float32)
    if shards:
        values = values * steps_of(key, shape, shards, -0.22, 0.18)
    return jnp.clip(raised(values, jax.random.fold_in(key, 3), *heavy), -most, most).astype(dtype)


def setup_inputs(seed: int = 0) -> dict:
    arg_keys = jax.random.split(jax.random.key(seed), 13)
    return {
        "grads_pair": heavy_noise(arg_keys[0], (WORKERS, 2, ROWS, FF), 1.0, 24.0, ((0, 128),), (0, 3, 128, 5.5)),
        "grads_down": heavy_noise(arg_keys[1], (WORKERS, DROWS, D), 1.0, 24.0, ((0, 128),), (0, 2, 128, 5.5)),
        "inner_pair": gaussian(arg_keys[2], (N_REPLICA, 2, ROWS, FF), 1.0, 6.0, ((0, 8), (3, 16)), jnp.float32),
        "inner_down": gaussian(arg_keys[3], (N_REPLICA, DROWS, D), 1.0, 6.0, ((0, 8), (2, 16)), jnp.float32),
        "first_pair": gaussian(arg_keys[4], (N_REPLICA, 2, ROWS, FF), 0.4, 2.4, ((0, 8), (3, 16)), jnp.float32),
        "first_down": gaussian(arg_keys[5], (N_REPLICA, DROWS, D), 0.4, 2.4, ((0, 8), (2, 16)), jnp.float32),
        "second_pair": jnp.clip(jnp.exp(math.log(2.0) - 2.9957323 * jax.random.uniform(arg_keys[6], (N_REPLICA, 2, ROWS, FF), jnp.float32) ** steps_of(arg_keys[6], (N_REPLICA, 2, ROWS, FF), ((0, 8), (3, 16)), -0.2, 0.2)), 0.1, 2.0),
        "second_down": jnp.clip(jnp.exp(math.log(2.0) - 2.9957323 * jax.random.uniform(arg_keys[7], (N_REPLICA, DROWS, D), jnp.float32) ** steps_of(arg_keys[7], (N_REPLICA, DROWS, D), ((0, 8), (2, 16)), -0.2, 0.2)), 0.1, 2.0),
        "anchor_pair": gaussian(arg_keys[8], (2, ROWS, FF), 1.0, 6.0, ((2, 16),), jnp.float32),
        "anchor_down": gaussian(arg_keys[9], (DROWS, D), 1.0, 6.0, ((1, 16),), jnp.float32),
        "velocity_pair": gaussian(arg_keys[10], (2, ROWS, FF), 0.3, 1.8, ((2, 16),), jnp.float32),
        "velocity_down": gaussian(arg_keys[11], (DROWS, D), 0.3, 1.8, ((1, 16),), jnp.float32),
    }


beta_one = 0.9
beta_two = 0.95
inner_rate = 0.2
decay_rate = 0.1
outer_rate = 0.7
momentum_keep = 0.9
epsilon_add = 1e-08

def inner_update(summed, inner, first, second):
    first_new = beta_one * first + (1.0 - beta_one) * summed
    second_new = beta_two * second + (1.0 - beta_two) * summed * summed
    first_fix = 1.0 - beta_one ** INNER_STEP
    second_fix = 1.0 - beta_two ** INNER_STEP
    ratio = first_new / first_fix / (jnp.sqrt(second_new / second_fix) + epsilon_add)
    return inner - inner_rate * (ratio + decay_rate * inner)

def family(grads, inner, first, second, anchor, velocity):
    grouped = grads.reshape((N_REPLICA, N_ZERO) + grads.shape[1:])

    def replica_step(running, pieces):
        grad_group, inner_one, first_one, second_one = pieces
        summed = lax.optimization_barrier(jnp.sum(grad_group.astype(jnp.float32), axis=0))
        inner_new = inner_update(summed, inner_one, first_one, second_one)
        return (running + (anchor - inner_new), None)
    running, _ = lax.scan(replica_step, jnp.zeros_like(anchor), (grouped, inner, first, second))
    pseudo = running / N_REPLICA
    velocity_next = momentum_keep * velocity + pseudo
    anchor_next = anchor - outer_rate * (pseudo + momentum_keep * velocity_next)
    return (anchor_next.astype(jnp.bfloat16), anchor_next, velocity_next)

def reference(grads_pair, grads_down, inner_pair, inner_down, first_pair, first_down, second_pair, second_down, anchor_pair, anchor_down, velocity_pair, velocity_down):
    weights_pair, anchor_pair_next, velocity_pair_next = family(grads_pair, inner_pair, first_pair, second_pair, anchor_pair, velocity_pair)
    weights_down, anchor_down_next, velocity_down_next = family(grads_down, inner_down, first_down, second_down, anchor_down, velocity_down)
    return (weights_pair, weights_down, anchor_pair_next, anchor_down_next, velocity_pair_next, velocity_down_next)
```

```python
import jax
import jax.numpy as jnp
from jax import lax
from jax.experimental import pallas as pl
from jax.experimental.pallas import tpu as pltpu
from jax.sharding import PartitionSpec as P

MESH = pl.DeviceIdType.MESH
BF = jnp.bfloat16
F32 = jnp.float32

INNER_STEP = 500
beta_one = 0.9
beta_two = 0.95
inner_rate = 0.2
decay_rate = 0.1
outer_rate = 0.7
momentum_keep = 0.9
epsilon_add = 1e-08

WIDE = {"p": 1792, "d": 512}
ROWS = 128

UNITS = [
    ("x", 0, [("p", 0, 256)]),
    ("y", 0, [("p", 1024, 256), ("d", 0, 128)]),
    ("x", 1, [("p", 256, 384)]),
    ("y", 1, [("p", 1280, 256), ("d", 128, 128)]),
    ("x", 2, [("p", 640, 384)]),
    ("y", 2, [("p", 1536, 256), ("d", 256, 256)]),
]
GATHER_LIST = [
    (0, 0, 256, "yxz"),
    (0, 256, 256, "xzy"),
    (0, 512, 128, "xyz"),
    (1, 0, 512, "yxz"),
    (1, 512, 256, "zxy"),
    (2, 0, 256, "zyx"),
    (2, 256, 384, "zyx"),
    (2, 640, 256, "xzy"),
]
GREET, MEET, CORE, LOAD, ROWS_IN, BASE, STATES, MIX, PX, FIRST, SECOND, CROSS, THIRD, BACK, FINAL, SUM, REPL, FAR, ALL, GATHER, DRAIN = range(21)
SCHEDULE = [
    (GREET,), (MEET,), (CORE, 0), (LOAD, 0), (CORE, 1), (LOAD, 2), (LOAD, 1),
    (CORE, 2), (MIX, 0), (PX, 0), (MIX, 1), (CORE, 5), (FIRST, 1), (MIX, 2),
    (LOAD, 5), (PX, 2), (BASE,), (SECOND, 1), (CORE, 3), (MIX, 5), (LOAD, 3),
    (CORE, 4), (FIRST, 5), (MIX, 3), (FIRST, 3), (THIRD, 1), (LOAD, 4), (CROSS, 0),
    (BACK, 1), (MIX, 4), (STATES, 1), (PX, 4), (FIRST, 0), (ROWS_IN,), (SECOND, 5),
    (STATES, 2), (SECOND, 3), (STATES, 3), (SUM,), (FINAL, 1), (SECOND, 0), (CROSS, 2),
    (STATES, 4), (REPL, 1), (FIRST, 2), (STATES, 0), (CROSS, 4), (THIRD, 5), (THIRD, 3),
    (STATES, 5), (FIRST, 4), (BACK, 3), (THIRD, 0), (SECOND, 2), (BACK, 5), (ALL,),
    (FAR, 1), (SECOND, 4), (GATHER, 0, 1), (REPL, 0), (GATHER, 0, 2), (FINAL, 3), (THIRD, 2),
    (THIRD, 4), (FINAL, 5), (REPL, 3), (GATHER, 1, 2), (FAR, 0), (REPL, 2), (GATHER, 0, 0),
    (GATHER, 1, 1), (REPL, 4), (FAR, 3), (GATHER, 2, 2), (REPL, 5), (FAR, 2), (GATHER, 1, 0),
    (GATHER, 0, 3), (FAR, 4), (GATHER, 0, 5), (GATHER, 2, 1), (GATHER, 0, 4), (FAR, 5), (GATHER, 0, 6),
    (GATHER, 0, 7), (GATHER, 1, 3), (GATHER, 2, 0), (GATHER, 1, 4), (GATHER, 1, 5), (GATHER, 1, 6), (GATHER, 1, 7),
    (GATHER, 2, 5), (GATHER, 3, 1), (GATHER, 4, 1), (GATHER, 2, 3), (GATHER, 3, 2), (GATHER, 4, 2), (GATHER, 3, 0),
    (GATHER, 4, 0), (GATHER, 2, 7), (GATHER, 2, 6), (GATHER, 3, 5), (GATHER, 4, 5), (GATHER, 5, 1), (GATHER, 2, 4),
    (GATHER, 6, 1), (GATHER, 3, 7), (GATHER, 4, 7), (GATHER, 3, 3), (GATHER, 4, 3), (GATHER, 3, 6), (GATHER, 4, 6),
    (GATHER, 3, 4), (GATHER, 4, 4), (GATHER, 5, 0), (GATHER, 5, 7), (GATHER, 5, 5), (GATHER, 5, 2), (GATHER, 5, 6),
    (GATHER, 5, 3), (GATHER, 6, 0), (GATHER, 5, 4), (GATHER, 6, 4), (GATHER, 6, 3), (GATHER, 6, 2), (GATHER, 6, 7),
    (GATHER, 6, 5), (GATHER, 6, 6), (DRAIN,),
]

WIDTHS = [sum(w for _, _, w in parts) for _, _, parts in UNITS]
CHUNKS = 1 + max(chunk for _, chunk, _ in UNITS)
CHUNK_WIDTHS = [sum(w for w, u in zip(WIDTHS, UNITS) if u[1] == k) for k in range(CHUNKS)]
TOTAL = sum(WIDTHS)


def unit_start(u):
    return sum(WIDTHS[v] for v in range(u) if UNITS[v][1] == UNITS[u][1])


def part_starts(u):
    at, out = 0, []
    for fam, off, w in UNITS[u][2]:
        out.append((fam, off, w, at))
        at += w
    return out


def natural(fam, off):
    return off if fam == "p" else WIDE["p"] + off


def inner_step(summed, first, second):
    first_new = beta_one * first + (1.0 - beta_one) * summed
    second_new = beta_two * second + (1.0 - beta_two) * summed * summed
    first_fix = 1.0 - beta_one**INNER_STEP
    second_fix = 1.0 - beta_two**INNER_STEP
    ratio = first_new / first_fix / (jnp.sqrt(second_new / second_fix) + epsilon_add)
    return inner_rate * ratio


class Scratch:
    def __init__(self):
        self.names, self.shapes = [], []

    def add(self, name, shape, dtype):
        self.names.append(name)
        self.shapes.append(pltpu.VMEM(shape, dtype))


def make_scratch():
    s = Scratch()
    for u, (kind, _, _) in enumerate(UNITS):
        w = WIDTHS[u]
        s.add(("own", u), (2, 4, ROWS, w), BF)
        s.add(("got", u), (2, 4, ROWS, w), BF)
        if kind == "x":
            s.add(("px", u), (4, ROWS, w), BF)
        else:
            s.add(("bx", u), (ROWS, w), BF)
        lead = () if kind == "x" else (2,)
        for name in ("t1p", "t1m", "f1p", "f1m", "f2p", "f2m"):
            s.add((name, u), lead + (ROWS // 2, w), BF)
        for name in ("first", "second"):
            s.add((name, u), (ROWS, w), F32)
        s.add(("sent", u), (2, 4, 16, w), BF)
        s.add(("repl", u), (3, 2, 16, w), BF)
        s.add(("part", u), (2, 16, w), BF)
        s.add(("far", u), (16, w), BF)
    for k in range(CHUNKS):
        s.add(("fresh", k), (16, CHUNK_WIDTHS[k]), BF)
    for name in ("anchor", "velocity", "all"):
        s.add(name, (16, TOTAL), F32)
    s.add("mine", (2, 16, TOTAL), F32)
    s.add("base", (3, 2, 16, TOTAL), F32)
    s.add("faraway", (16, TOTAL), F32)
    return s


N_SEM = 700


def step_kernel(names, *refs):
    grads = {"p": refs[0], "d": refs[1]}
    states = {
        "inner": {"p": refs[2], "d": refs[3]},
        "first": {"p": refs[4], "d": refs[5]},
        "second": {"p": refs[6], "d": refs[7]},
        "anchor": {"p": refs[8], "d": refs[9]},
        "velocity": {"p": refs[10], "d": refs[11]},
    }
    n_gather = len(GATHER_LIST)
    full = refs[12 : 12 + n_gather]
    outer = refs[12 + n_gather]
    rest = refs[13 + n_gather :]
    buf = dict(zip(names, rest))
    sems = rest[len(names)]
    count = [0]

    def sem():
        count[0] += 1
        assert count[0] <= N_SEM
        return sems.at[count[0] - 1]

    rep, zero = lax.axis_index("replica"), lax.axis_index("zero")
    xh, z = lax.div(rep, 4), lax.rem(rep, 4)
    xl, y, c = lax.div(zero, 8), lax.rem(lax.div(zero, 2), 4), lax.rem(zero, 2)
    x = xh * 2 + xl
    here = {"x": x, "y": y, "z": z}

    def place(x, y, z, c):
        return (lax.div(x, 2) * 4 + z, (lax.rem(x, 2) * 4 + y) * 2 + c)

    def near(dim, by):
        at = dict(here)
        at[dim] = lax.rem(at[dim] + by + 4, 4)
        return place(at["x"], at["y"], at["z"], c)

    sibling = place(x, y, z, 1 - c)
    pair = place(xh * 2 + 1 - xl, y, z, c)
    opposite = near("x", 2)

    def other(by):
        return lax.rem(y + by + 4, 4)

    live = {}

    def send(key, src, dst, device):
        copy = pltpu.make_async_remote_copy(
            src_ref=src, dst_ref=dst, send_sem=sem(), recv_sem=sem(), device_id=device, device_id_type=MESH
        )
        copy.start()
        live[key] = copy
        pending.append(key)

    pending, unread = [], []

    def arrive(key):
        live[key].wait_recv()
        pending.remove(key)

    local = {}

    def replica_rows(name, r, target):
        out = []
        for g in range(2):
            src = states[name]["p"].at[pl.ds(pl.multiple_of(g * 64 + r * 8, 8), 8)]
            out.append((src, target.at[pl.ds(g * 8, 8), pl.ds(0, WIDE["p"])]))
        src = states[name]["d"].at[pl.ds(pl.multiple_of(r * 16, 16), 16)]
        out.append((src, target.at[:, pl.ds(WIDE["p"], WIDE["d"])]))
        return out

    def load(u):
        mine = local["own", u] = sem()
        unread.append(("own", u))
        for fam, off, w, at in part_starts(u):

            @pl.loop(0, 8)
            def _(d, fam=fam, off=off, w=w, at=at):
                col = pl.multiple_of((d * 2 + c) * WIDE[fam] + off, 128)
                pltpu.make_async_copy(
                    grads[fam].at[:, pl.ds(col, w)],
                    buf["own", u].at[lax.div(d, 4), lax.rem(d, 4), :, pl.ds(at, w)],
                    mine,
                ).start()

    def load_states(u):
        for name in ("first", "second"):
            s = local[name, u] = sem()
            unread.append((name, u))
            for fam, off, w, at in part_starts(u):
                pltpu.make_async_copy(
                    states[name][fam].at[:, pl.ds(off, w)], buf[name, u].at[:, pl.ds(at, w)], s
                ).start()

    def load_rows():
        for name in ("anchor", "velocity"):
            s = local[name] = sem()
            unread.append(name)
            for src, dst in replica_rows(name, rep, buf[name]):
                pltpu.make_async_copy(src, dst, s).start()

    def base_send():
        for by in (1, 2, 3):
            out, into = sem(), sem()
            for b in range(2):
                for src, dst in replica_rows("inner", b * 4 + lax.rem(z + by, 4), buf["base"].at[by - 1, b]):
                    pltpu.make_async_remote_copy(
                        src_ref=src, dst_ref=dst, send_sem=out, recv_sem=into,
                        device_id=near("z", by), device_id_type=MESH,
                    ).start()
            whole = buf["base"].at[by - 1]
            live["base", by] = pltpu.make_async_remote_copy(
                src_ref=whole, dst_ref=whole, send_sem=out, recv_sem=into, device_id=near("z", by), device_id_type=MESH
            )
            pending.append(("base", by))
        s = local["mine"] = sem()
        unread.append("mine")
        for b in range(2):
            for src, dst in replica_rows("inner", b * 4 + z, buf["mine"].at[b]):
                pltpu.make_async_copy(src, dst, s).start()

    def base_sum():
        loaded("mine")
        for by in (1, 2, 3):
            arrive(("base", by))
        mine, got = buf["mine"], buf["base"]

        @pl.loop(0, TOTAL // 256)
        def _(i):
            cols = pl.ds(pl.multiple_of(i * 256, 256), 256)
            for b in range(2):
                mine[b, :, cols] = mine[b, :, cols] + got[0, b, :, cols] + got[1, b, :, cols] + got[2, b, :, cols]

        send("faraway", mine.at[1 - xh], buf["faraway"], opposite)

    def base_all():
        arrive("faraway")
        loaded("anchor")
        loaded("velocity")

        @pl.loop(0, TOTAL // 256)
        def _(i):
            cols = pl.ds(pl.multiple_of(i * 256, 256), 256)
            kept = (1.0 - inner_rate * decay_rate) / 8.0
            buf["all"][:, cols] = kept * (buf["mine"][xh, :, cols] + buf["faraway"][:, cols])

    def loaded(key):
        pltpu.make_async_copy(buf[key], buf[key], local[key]).wait()
        unread.remove(key)

    friends = [sibling] + [near(dim, by) for dim in "xyz" for by in (1, 2, 3)]
    gate = pltpu.get_barrier_semaphore()

    def greet():
        for friend in friends:
            pl.semaphore_signal(gate, inc=1, device_id=friend, device_id_type=MESH)

    def meet():
        pl.semaphore_wait(gate, len(friends))

    def core(u):
        out, into = sem(), sem()
        for fam, off, w, at in part_starts(u):

            @pl.loop(0, 8)
            def _(d, fam=fam, off=off, w=w, at=at):
                col = pl.multiple_of((d * 2 + 1 - c) * WIDE[fam] + off, 128)
                pltpu.make_async_remote_copy(
                    src_ref=grads[fam].at[:, pl.ds(col, w)],
                    dst_ref=buf["got", u].at[lax.div(d, 4), lax.rem(d, 4), :, pl.ds(at, w)],
                    send_sem=out,
                    recv_sem=into,
                    device_id=sibling,
                    device_id_type=MESH,
                ).start()
        live["core", u] = pltpu.make_async_remote_copy(
            src_ref=buf["got", u],
            dst_ref=buf["got", u],
            send_sem=out,
            recv_sem=into,
            device_id=sibling,
            device_id_type=MESH,
        )
        pending.append(("core", u))

    def add_rows(dst, src, rows):
        @pl.loop(0, rows // 32)
        def _(i):
            at = pl.ds(pl.multiple_of(i * 32, 32), 32)
            dst[at, :] = dst[at, :] + src[at, :]

    def add_blocks(own, got, xl_at):
        @pl.loop(0, 4 * ROWS // 32)
        def _(i):
            b, at = lax.div(i, 4), pl.ds(pl.multiple_of(lax.rem(i, 4) * 32, 32), 32)
            own[xl_at, b, at, :] = own[xl_at, b, at, :] + got[xl_at, b, at, :]

    def mix(u):
        loaded(("own", u))
        arrive(("core", u))
        own, got = buf["own", u], buf["got", u]
        add_blocks(own, got, 1 - xl)
        add_blocks(own, got, xl)

    def send_pair(u):
        send(("px", u), buf["own", u].at[1 - xl], buf["px", u], pair)

    def cross(u):
        arrive(("px", u))
        own, px = buf["own", u], buf["px", u]

        @pl.loop(0, 4 * ROWS // 32)
        def _(i):
            b, at = lax.div(i, 4), pl.ds(pl.multiple_of(lax.rem(i, 4) * 32, 32), 32)
            own[xl, b, at, :] = own[xl, b, at, :] + px[b, at, :]

    half = ROWS // 2
    low, high = pl.ds(0, half), pl.ds(half, half)

    def block(u, at, rows):
        own = buf["own", u]
        return own.at[xl, at, rows] if UNITS[u][0] == "x" else own.at[:, at, rows]

    def first(u):
        send(("t1p", u), block(u, other(2), low), buf["t1p", u], near("y", 1))
        send(("t1m", u), block(u, other(2), high), buf["t1m", u], near("y", -1))
        send(("f1p", u), block(u, other(1), high), buf["f1p", u], near("y", 1))
        send(("f1m", u), block(u, other(-1), low), buf["f1m", u], near("y", -1))

    def add_into(u, at, start, src):
        own = buf["own", u]
        if UNITS[u][0] == "x":
            add_rows(own.at[xl, at, pl.ds(start, half)], src, half)
        else:
            for i in range(2):
                add_rows(own.at[i, at, pl.ds(start, half)], src.at[i], half)

    def second(u):
        arrive(("t1p", u))
        add_into(u, other(1), 0, buf["t1p", u])
        send(("f2p", u), block(u, other(1), low), buf["f2p", u], near("y", 1))
        arrive(("t1m", u))
        add_into(u, other(-1), half, buf["t1m", u])
        send(("f2m", u), block(u, other(-1), high), buf["f2m", u], near("y", -1))

    def update(u, h, t, summed):
        at = pl.ds(pl.multiple_of(h * half + t * 16, 16), 16)
        new = inner_step(summed, buf["first", u][at, :], buf["second", u][at, :])
        sent = buf["sent", u]
        for fam, _, w, start in part_starts(u):
            cols = pl.ds(start, w)
            piece = new[:, start : start + w]
            if fam == "p":
                sent[lax.div(t, 2), 2 * lax.rem(t, 2), h * 8 : h * 8 + 8, cols] = piece[:8].astype(BF)
                sent[lax.div(t, 2), 2 * lax.rem(t, 2) + 1, h * 8 : h * 8 + 8, cols] = piece[8:].astype(BF)
            else:
                sent[h, t, :, cols] = piece.astype(BF)

    def states_ready(u):
        for name in ("first", "second"):
            loaded((name, u))

    def third(u):
        for name in ("f1p", "f1m", "f2p", "f2m"):
            arrive((name, u))
        own = buf["own", u]
        if UNITS[u][0] == "x":
            states_ready(u)
        for h, (one, two) in enumerate((("f2p", "f1m"), ("f1p", "f2m"))):
            if UNITS[u][0] == "x":

                @pl.loop(0, 4)
                def _(t, h=h, one=one, two=two):
                    at = pl.ds(pl.multiple_of(t * 16, 16), 16)
                    mine = own[xl, y, pl.ds(pl.multiple_of(h * half + t * 16, 16), 16), :].astype(F32)
                    total = mine + buf[one, u][at, :].astype(F32) + buf[two, u][at, :].astype(F32)
                    update(u, h, t, total)
            else:

                @pl.loop(0, 8)
                def _(i, h=h, one=one, two=two):
                    b, t = lax.div(i, 4), lax.rem(i, 4)
                    at = pl.ds(pl.multiple_of(t * 16, 16), 16)
                    to = pl.ds(pl.multiple_of(h * half + t * 16, 16), 16)
                    total = own[b, y, to, :].astype(F32) + buf[one, u][b, at, :].astype(F32)
                    own[b, y, to, :] = (total + buf[two, u][b, at, :].astype(F32)).astype(BF)
        if UNITS[u][0] == "x":
            spread(u)

    def back(u):
        send(("bx", u), buf["own", u].at[1 - xl, y], buf["bx", u], pair)

    def final(u):
        arrive(("bx", u))
        states_ready(u)
        own, bx = buf["own", u], buf["bx", u]
        for h in range(2):

            @pl.loop(0, 4)
            def _(t, h=h):
                at = pl.ds(pl.multiple_of(h * half + t * 16, 16), 16)
                update(u, h, t, own[xl, y, at, :].astype(F32) + bx[at, :].astype(F32))

        spread(u)

    def spread(u):
        for by in (1, 2, 3):
            send(("repl", u, by), buf["sent", u].at[:, lax.rem(z + by, 4)], buf["repl", u].at[by - 1], near("z", by))

    def repl(u):
        for by in (1, 2, 3):
            arrive(("repl", u, by))
        sent, got, part = buf["sent", u], buf["repl", u], buf["part", u]
        for b in (1 - xh, xh):
            total = sent[b, z].astype(F32) + got[0, b].astype(F32) + got[1, b].astype(F32) + got[2, b].astype(F32)
            part[b] = total.astype(BF)
        send(("far", u), part.at[1 - xh], buf["far", u], opposite)

    def far(u):
        arrive(("far", u))
        for fam, off, w, at in part_starts(u):
            cols, to = pl.ds(at, w), pl.ds(natural(fam, off), w)
            steps = buf["part", u][xh, :, cols].astype(F32) + buf["far", u][:, cols].astype(F32)
            anchor = buf["anchor"][:, to]
            pseudo = anchor - (buf["all"][:, to] - steps / 8.0)
            velocity_next = momentum_keep * buf["velocity"][:, to] + pseudo
            anchor_next = anchor - outer_rate * (pseudo + momentum_keep * velocity_next)
            outer[0, :, to] = anchor_next
            outer[1, :, to] = velocity_next
            buf["fresh", UNITS[u][1]][:, pl.ds(unit_start(u) + at, w)] = anchor_next.astype(BF)

    def slot(dim, by=0):
        at = lax.rem(here[dim] + by + 4, 4)
        return lax.rem(at, 2) * 2 + lax.div(at, 2) if dim == "x" else at

    def gather(stage, g):
        k, at, w, (d1, d2, d3) = GATHER_LIST[g]
        whole = full[g]
        if stage == 0:
            mine = whole.at[c, slot(d3), slot(d2), slot(d1)]
            mine[...] = buf["fresh", k][:, pl.ds(at, w)]
            for by in (1, 3, 2):
                send(("g", g, "0", by), mine, mine, near(d1, by))
        elif stage == 1:
            for by in (1, 3, 2):
                arrive(("g", g, "0", by))
            mine = whole.at[c, slot(d3), slot(d2)]
            for by in (1, 3, 2):
                send(("g", g, "1", by), mine, mine, near(d2, by))
        elif stage == 2:
            for by in (1, 3, 2):
                arrive(("g", g, "1", by))
            for turn in (0, 1):
                for by, part in ((1, 0), (3, 2)):
                    some = whole.at[c, slot(d3), pl.ds(part if turn == 0 else 2 - part, 2)]
                    send(("g", g, "2", by, turn), some, some, near(d3, by))
            mine = whole.at[c, slot(d3)]
            send(("g", g, "s", 0), mine, mine, sibling)
        elif stage == 3:
            for by, part in ((1, 0), (3, 2)):
                arrive(("g", g, "2", by, 0))
                some = whole.at[c, slot(d3, -by), pl.ds(part, 2)]
                send(("g", g, "3", by), some, some, near(d3, by))
        elif stage == 4:
            for by in (1, 3):
                arrive(("g", g, "2", by, 1))
                got = whole.at[c, slot(d3, -by)]
                send(("g", g, "s", by), got, got, sibling)
        elif stage == 5:
            for by, part in ((1, 0), (3, 2)):
                arrive(("g", g, "3", by))
                some = whole.at[c, slot(d3, 2), pl.ds(part, 2)]
                send(("g", g, "t", by), some, some, sibling)
        else:
            for key in (("s", 0), ("s", 1), ("s", 3), ("t", 1), ("t", 3)):
                arrive(("g", g) + key)

    def drain():
        for key in list(pending):
            arrive(key)
        for key in list(unread):
            loaded(key)
        for copy in live.values():
            copy.wait_send()

    acts = {
        GREET: greet, MEET: meet, CORE: core, LOAD: load, ROWS_IN: load_rows, BASE: base_send, STATES: load_states,
        MIX: mix, PX: send_pair, FIRST: first, SECOND: second, CROSS: cross, THIRD: third, BACK: back, FINAL: final,
        SUM: base_sum, REPL: repl, FAR: far, ALL: base_all, GATHER: gather, DRAIN: drain,
    }
    for act, *where in SCHEDULE:
        acts[act](*where)


def gather_shape(g):
    _, _, w, _ = GATHER_LIST[g]
    return (2, 4, 4, 4, 16, w)


def run_step(args):
    s = make_scratch()
    outs = [pltpu.VMEM(gather_shape(g), BF) for g in range(len(GATHER_LIST))]
    outs.append(pltpu.VMEM((2, 16, TOTAL), F32))

    def kernel(*refs):
        step_kernel(s.names, *refs)

    return pl.pallas_call(
        kernel,
        out_shape=outs,
        in_specs=[pl.BlockSpec(memory_space=pltpu.HBM)] * 12,
        out_specs=[pl.BlockSpec(memory_space=pltpu.VMEM)] * len(outs),
        scratch_shapes=s.shapes + [pltpu.SemaphoreType.DMA((N_SEM,))],
        compiler_params=pltpu.CompilerParams(
            collective_id=0, has_side_effects=True, vmem_limit_bytes=48 * 2**20
        ),
        name="outer_step",
    )(*args)


def column_pieces():
    out = []
    for g, (k, at, w, _) in enumerate(GATHER_LIST):
        for u in range(len(UNITS)):
            if UNITS[u][1] != k:
                continue
            for fam, off, wide, start in part_starts(u):
                begin = unit_start(u) + start
                lo, hi = max(begin, at), min(begin + wide, at + w)
                if lo < hi:
                    out.append((g, lo - at, hi - lo, fam, off + lo - begin))
    return out


def place_kernel(*refs):
    n = len(GATHER_LIST)
    full, outer = refs[:n], refs[n]
    weights_pair, weights_down, anchor_pair, anchor_down, velocity_pair, velocity_down = refs[n + 1 : n + 7]
    pair_rows, down_rows, sems = refs[n + 7 :]

    for i, (pair, down) in enumerate(((anchor_pair, anchor_down), (velocity_pair, velocity_down))):
        pair[0] = outer[i, :8, : WIDE["p"]]
        pair[1] = outer[i, 8:, : WIDE["p"]]
        down[...] = outer[i, :, WIDE["p"] :]

    @pl.loop(0, 16)
    def _(q):
        c, y, xl = lax.rem(q, 2), lax.rem(lax.div(q, 2), 4), lax.div(q, 8)

        def block(g, r):
            index = {"x": xl * 2 + r // 4, "y": y, "z": r % 4}
            return (c,) + tuple(index[d] for d in reversed(GATHER_LIST[g][3]))

        start = {fam: pl.multiple_of(q * WIDE[fam], 128) for fam in WIDE}
        for g, at, w, fam, col in column_pieces():
            to = pl.ds(pl.multiple_of(start[fam] + col, 128), w)
            for m in range(4):
                one = full[g][block(g, 2 * m) + (slice(None), slice(at, at + w))]
                two = full[g][block(g, 2 * m + 1) + (slice(None), slice(at, at + w))]
                if fam == "d":
                    down_rows[32 * m : 32 * m + 16, to] = one
                    down_rows[32 * m + 16 : 32 * m + 32, to] = two
                else:
                    for half in range(2):
                        rows = slice(8 * half, 8 * half + 8)
                        pair_rows[half, 16 * m : 16 * m + 16, to] = jnp.concatenate([one[rows], two[rows]], axis=0)
        cols = pl.ds(start["p"], WIDE["p"])
        pltpu.make_async_copy(pair_rows.at[:, :, cols], weights_pair.at[:, :, cols], sems.at[0]).start()
        cols = pl.ds(start["d"], WIDE["d"])
        pltpu.make_async_copy(down_rows.at[:, cols], weights_down.at[:, cols], sems.at[1]).start()

    pltpu.make_async_copy(pair_rows, weights_pair, sems.at[0]).wait()
    pltpu.make_async_copy(down_rows, weights_down, sems.at[1]).wait()


def run_place(full, outer):
    vmem = pl.BlockSpec(memory_space=pltpu.VMEM)
    hbm = pl.BlockSpec(memory_space=pltpu.HBM)
    return pl.pallas_call(
        place_kernel,
        out_shape=[
            jax.ShapeDtypeStruct((2, 64, 28672), BF),
            jax.ShapeDtypeStruct((128, 8192), BF),
            jax.ShapeDtypeStruct((2, 8, 1792), F32),
            jax.ShapeDtypeStruct((16, 512), F32),
            jax.ShapeDtypeStruct((2, 8, 1792), F32),
            jax.ShapeDtypeStruct((16, 512), F32),
        ],
        in_specs=[vmem] * (len(full) + 1),
        out_specs=[hbm, hbm, vmem, vmem, vmem, vmem],
        scratch_shapes=[
            pltpu.VMEM((2, 64, 28672), BF),
            pltpu.VMEM((128, 8192), BF),
            pltpu.SemaphoreType.DMA((2,)),
        ],
        compiler_params=pltpu.CompilerParams(vmem_limit_bytes=32 * 2**20),
        name="place",
    )(*full, outer)


def body(
    grads_pair,
    grads_down,
    inner_pair,
    inner_down,
    first_pair,
    first_down,
    second_pair,
    second_down,
    anchor_pair,
    anchor_down,
    velocity_pair,
    velocity_down,
):
    args = [
        grads_pair.reshape(128, 28672),
        grads_down.reshape(128, 8192),
        inner_pair.reshape(128, 1792),
        inner_down.reshape(128, 512),
        first_pair.reshape(128, 1792),
        first_down.reshape(128, 512),
        second_pair.reshape(128, 1792),
        second_down.reshape(128, 512),
        anchor_pair.reshape(128, 1792),
        anchor_down,
        velocity_pair.reshape(128, 1792),
        velocity_down,
    ]
    *full, outer = run_step(args)
    return tuple(run_place(full, outer))


def solution(mesh):
    in_specs = (
        P(("replica", "zero"), None, None, None),
        P(("replica", "zero"), None, None),
        P("replica", None, None, "zero"),
        P("replica", None, "zero"),
        P("replica", None, None, "zero"),
        P("replica", None, "zero"),
        P("replica", None, None, "zero"),
        P("replica", None, "zero"),
        P(None, None, "zero"),
        P(None, "zero"),
        P(None, None, "zero"),
        P(None, "zero"),
    )
    out_specs = (
        P(),
        P(),
        P(None, "replica", "zero"),
        P("replica", "zero"),
        P(None, "replica", "zero"),
        P("replica", "zero"),
    )
    return jax.shard_map(body, mesh=mesh, in_specs=in_specs, out_specs=out_specs, check_vma=False)
```

```python
import jax
import jax.numpy as jnp
from jax import lax
from jax.experimental import pallas as pl
from jax.experimental.pallas import tpu as pltpu
from jax.sharding import PartitionSpec as P

MESH = pl.DeviceIdType.MESH
BF = jnp.bfloat16
F32 = jnp.float32

INNER_STEP = 500
beta_one = 0.9
beta_two = 0.95
inner_rate = 0.2
decay_rate = 0.1
outer_rate = 0.7
momentum_keep = 0.9
epsilon_add = 1e-08

WIDE = {"p": 1792, "d": 512}
ROWS = 128

UNITS = [
    ("x", 0, [("p", 0, 256)]),
    ("y", 0, [("p", 1024, 256), ("d", 0, 128)]),
    ("x", 1, [("p", 256, 384)]),
    ("y", 1, [("p", 1280, 256), ("d", 128, 128)]),
    ("x", 2, [("p", 640, 384)]),
    ("y", 2, [("p", 1536, 256), ("d", 256, 256)]),
]
GATHER_LIST = [
    (0, 0, 256, "yxz"),
    (0, 256, 256, "xzy"),
    (0, 512, 128, "xyz"),
    (1, 0, 512, "yxz"),
    (1, 512, 256, "zxy"),
    (2, 0, 256, "zyx"),
    (2, 256, 384, "zyx"),
    (2, 640, 256, "xzy"),
]
GREET, MEET, CORE, LOAD, ROWS_IN, BASE, STATES, MIX, PX, FIRST, SECOND, CROSS, THIRD, BACK, FINAL, SUM, REPL, FAR, ALL, GATHER, DRAIN = range(21)
SCHEDULE = [
    (GREET,), (MEET,), (CORE, 0), (LOAD, 0), (CORE, 1), (LOAD, 2), (LOAD, 1),
    (CORE, 2), (MIX, 0), (PX, 0), (MIX, 1), (CORE, 5), (FIRST, 1), (MIX, 2),
    (BASE,), (LOAD, 5), (PX, 2), (SECOND, 1), (CORE, 3), (MIX, 5), (LOAD, 3),
    (CORE, 4), (FIRST, 5), (MIX, 3), (FIRST, 3), (THIRD, 1), (LOAD, 4), (CROSS, 0),
    (BACK, 1), (MIX, 4), (STATES, 1), (PX, 4), (FIRST, 0), (ROWS_IN,), (SECOND, 5),
    (STATES, 2), (SECOND, 3), (STATES, 3), (SUM,), (FINAL, 1), (SECOND, 0), (CROSS, 2),
    (STATES, 4), (REPL, 1), (FIRST, 2), (STATES, 0), (CROSS, 4), (THIRD, 5), (THIRD, 3),
    (STATES, 5), (FIRST, 4), (BACK, 3), (THIRD, 0), (SECOND, 2), (BACK, 5), (ALL,),
    (FAR, 1), (SECOND, 4), (GATHER, 0, 1), (REPL, 0), (GATHER, 0, 2), (FINAL, 3), (THIRD, 2),
    (THIRD, 4), (FINAL, 5), (REPL, 3), (GATHER, 1, 2), (FAR, 0), (REPL, 2), (GATHER, 0, 0),
    (GATHER, 1, 1), (REPL, 4), (FAR, 3), (GATHER, 2, 2), (REPL, 5), (FAR, 2), (GATHER, 1, 0),
    (GATHER, 0, 3), (FAR, 4), (GATHER, 0, 5), (GATHER, 2, 1), (GATHER, 0, 4), (FAR, 5), (GATHER, 0, 6),
    (GATHER, 0, 7), (GATHER, 1, 3), (GATHER, 2, 0), (GATHER, 1, 4), (GATHER, 1, 5), (GATHER, 1, 6), (GATHER, 1, 7),
    (GATHER, 2, 5), (GATHER, 3, 1), (GATHER, 4, 1), (GATHER, 2, 3), (GATHER, 3, 2), (GATHER, 4, 2), (GATHER, 3, 0),
    (GATHER, 4, 0), (GATHER, 2, 7), (GATHER, 2, 6), (GATHER, 3, 5), (GATHER, 4, 5), (GATHER, 5, 1), (GATHER, 2, 4),
    (GATHER, 6, 1), (GATHER, 3, 7), (GATHER, 4, 7), (GATHER, 3, 3), (GATHER, 4, 3), (GATHER, 3, 6), (GATHER, 4, 6),
    (GATHER, 3, 4), (GATHER, 4, 4), (GATHER, 5, 0), (GATHER, 5, 7), (GATHER, 5, 2), (GATHER, 5, 5), (GATHER, 5, 6),
    (GATHER, 5, 3), (GATHER, 6, 0), (GATHER, 5, 4), (GATHER, 6, 4), (GATHER, 6, 3), (GATHER, 6, 2), (GATHER, 6, 7),
    (GATHER, 6, 5), (GATHER, 6, 6), (DRAIN,),
]

WIDTHS = [sum(w for _, _, w in parts) for _, _, parts in UNITS]
CHUNKS = 1 + max(chunk for _, chunk, _ in UNITS)
CHUNK_WIDTHS = [sum(w for w, u in zip(WIDTHS, UNITS) if u[1] == k) for k in range(CHUNKS)]
TOTAL = sum(WIDTHS)


def unit_start(u):
    return sum(WIDTHS[v] for v in range(u) if UNITS[v][1] == UNITS[u][1])


def part_starts(u):
    at, out = 0, []
    for fam, off, w in UNITS[u][2]:
        out.append((fam, off, w, at))
        at += w
    return out


def natural(fam, off):
    return off if fam == "p" else WIDE["p"] + off


def inner_step(summed, first, second):
    first_new = beta_one * first + (1.0 - beta_one) * summed
    second_new = beta_two * second + (1.0 - beta_two) * summed * summed
    first_fix = 1.0 - beta_one**INNER_STEP
    second_fix = 1.0 - beta_two**INNER_STEP
    ratio = first_new / first_fix / (jnp.sqrt(second_new / second_fix) + epsilon_add)
    return inner_rate * ratio


class Scratch:
    def __init__(self):
        self.names, self.shapes = [], []

    def add(self, name, shape, dtype):
        self.names.append(name)
        self.shapes.append(pltpu.VMEM(shape, dtype))


def make_scratch():
    s = Scratch()
    for u, (kind, _, _) in enumerate(UNITS):
        w = WIDTHS[u]
        s.add(("own", u), (2, 4, ROWS, w), BF)
        s.add(("got", u), (2, 4, ROWS, w), BF)
        if kind == "x":
            s.add(("px", u), (4, ROWS, w), BF)
        else:
            s.add(("bx", u), (ROWS, w), BF)
        lead = () if kind == "x" else (2,)
        for name in ("t1p", "t1m", "f1p", "f1m", "f2p", "f2m"):
            s.add((name, u), lead + (ROWS // 2, w), BF)
        for name in ("first", "second"):
            s.add((name, u), (ROWS, w), F32)
        s.add(("sent", u), (2, 4, 16, w), BF)
        s.add(("repl", u), (3, 2, 16, w), BF)
        s.add(("part", u), (2, 16, w), BF)
        s.add(("far", u), (16, w), BF)
    for k in range(CHUNKS):
        s.add(("fresh", k), (16, CHUNK_WIDTHS[k]), BF)
    for name in ("anchor", "velocity", "all"):
        s.add(name, (16, TOTAL), F32)
    s.add("mine", (2, 16, TOTAL), F32)
    s.add("base", (3, 2, 16, TOTAL), F32)
    s.add("faraway", (16, TOTAL), F32)
    return s


N_SEM = 700


def step_kernel(names, *refs):
    grads = {"p": refs[0], "d": refs[1]}
    states = {
        "inner": {"p": refs[2], "d": refs[3]},
        "first": {"p": refs[4], "d": refs[5]},
        "second": {"p": refs[6], "d": refs[7]},
        "anchor": {"p": refs[8], "d": refs[9]},
        "velocity": {"p": refs[10], "d": refs[11]},
    }
    n_gather = len(GATHER_LIST)
    full = refs[12 : 12 + n_gather]
    outer = refs[12 + n_gather]
    rest = refs[13 + n_gather :]
    buf = dict(zip(names, rest))
    sems = rest[len(names)]
    count = [0]

    def sem():
        count[0] += 1
        assert count[0] <= N_SEM
        return sems.at[count[0] - 1]

    rep, zero = lax.axis_index("replica"), lax.axis_index("zero")
    xh, z = lax.div(rep, 4), lax.rem(rep, 4)
    xl, y, c = lax.div(zero, 8), lax.rem(lax.div(zero, 2), 4), lax.rem(zero, 2)
    x = xh * 2 + xl
    here = {"x": x, "y": y, "z": z}

    def place(x, y, z, c):
        return (lax.div(x, 2) * 4 + z, (lax.rem(x, 2) * 4 + y) * 2 + c)

    def near(dim, by):
        at = dict(here)
        at[dim] = lax.rem(at[dim] + by + 4, 4)
        return place(at["x"], at["y"], at["z"], c)

    sibling = place(x, y, z, 1 - c)
    pair = place(xh * 2 + 1 - xl, y, z, c)
    opposite = near("x", 2)

    def other(by):
        return lax.rem(y + by + 4, 4)

    live = {}

    def send(key, src, dst, device):
        copy = pltpu.make_async_remote_copy(
            src_ref=src, dst_ref=dst, send_sem=sem(), recv_sem=sem(), device_id=device, device_id_type=MESH
        )
        copy.start()
        live[key] = copy
        pending.append(key)

    pending, unread = [], []

    def arrive(key):
        live[key].wait_recv()
        pending.remove(key)

    local = {}

    def replica_rows(name, r, target):
        out = []
        for g in range(2):
            src = states[name]["p"].at[pl.ds(pl.multiple_of(g * 64 + r * 8, 8), 8)]
            out.append((src, target.at[pl.ds(g * 8, 8), pl.ds(0, WIDE["p"])]))
        src = states[name]["d"].at[pl.ds(pl.multiple_of(r * 16, 16), 16)]
        out.append((src, target.at[:, pl.ds(WIDE["p"], WIDE["d"])]))
        return out

    def load(u):
        mine = local["own", u] = sem()
        unread.append(("own", u))
        for fam, off, w, at in part_starts(u):

            @pl.loop(0, 8)
            def _(d, fam=fam, off=off, w=w, at=at):
                col = pl.multiple_of((d * 2 + c) * WIDE[fam] + off, 128)
                pltpu.make_async_copy(
                    grads[fam].at[:, pl.ds(col, w)],
                    buf["own", u].at[lax.div(d, 4), lax.rem(d, 4), :, pl.ds(at, w)],
                    mine,
                ).start()

    def load_states(u):
        for name in ("first", "second"):
            s = local[name, u] = sem()
            unread.append((name, u))
            for fam, off, w, at in part_starts(u):
                pltpu.make_async_copy(
                    states[name][fam].at[:, pl.ds(off, w)], buf[name, u].at[:, pl.ds(at, w)], s
                ).start()

    def load_rows():
        for name in ("anchor", "velocity"):
            s = local[name] = sem()
            unread.append(name)
            for src, dst in replica_rows(name, rep, buf[name]):
                pltpu.make_async_copy(src, dst, s).start()

    def base_send():
        for by in (1, 2, 3):
            out, into = sem(), sem()
            for b in range(2):
                for src, dst in replica_rows("inner", b * 4 + lax.rem(z + by, 4), buf["base"].at[by - 1, b]):
                    pltpu.make_async_remote_copy(
                        src_ref=src, dst_ref=dst, send_sem=out, recv_sem=into,
                        device_id=near("z", by), device_id_type=MESH,
                    ).start()
            whole = buf["base"].at[by - 1]
            live["base", by] = pltpu.make_async_remote_copy(
                src_ref=whole, dst_ref=whole, send_sem=out, recv_sem=into, device_id=near("z", by), device_id_type=MESH
            )
            pending.append(("base", by))
        s = local["mine"] = sem()
        unread.append("mine")
        for b in range(2):
            for src, dst in replica_rows("inner", b * 4 + z, buf["mine"].at[b]):
                pltpu.make_async_copy(src, dst, s).start()

    def base_sum():
        loaded("mine")
        for by in (1, 2, 3):
            arrive(("base", by))
        mine, got = buf["mine"], buf["base"]

        @pl.loop(0, TOTAL // 256)
        def _(i):
            cols = pl.ds(pl.multiple_of(i * 256, 256), 256)
            for b in range(2):
                mine[b, :, cols] = mine[b, :, cols] + got[0, b, :, cols] + got[1, b, :, cols] + got[2, b, :, cols]

        send("faraway", mine.at[1 - xh], buf["faraway"], opposite)

    def base_all():
        arrive("faraway")
        loaded("anchor")
        loaded("velocity")

        @pl.loop(0, TOTAL // 256)
        def _(i):
            cols = pl.ds(pl.multiple_of(i * 256, 256), 256)
            kept = (1.0 - inner_rate * decay_rate) / 8.0
            buf["all"][:, cols] = kept * (buf["mine"][xh, :, cols] + buf["faraway"][:, cols])

    def loaded(key):
        pltpu.make_async_copy(buf[key], buf[key], local[key]).wait()
        unread.remove(key)

    friends = [sibling] + [near(dim, by) for dim in "xyz" for by in (1, 2, 3)]
    gate = pltpu.get_barrier_semaphore()

    def greet():
        for friend in friends:
            pl.semaphore_signal(gate, inc=1, device_id=friend, device_id_type=MESH)

    def meet():
        pl.semaphore_wait(gate, len(friends))

    def core(u):
        out, into = sem(), sem()
        for fam, off, w, at in part_starts(u):

            @pl.loop(0, 8)
            def _(d, fam=fam, off=off, w=w, at=at):
                col = pl.multiple_of((d * 2 + 1 - c) * WIDE[fam] + off, 128)
                pltpu.make_async_remote_copy(
                    src_ref=grads[fam].at[:, pl.ds(col, w)],
                    dst_ref=buf["got", u].at[lax.div(d, 4), lax.rem(d, 4), :, pl.ds(at, w)],
                    send_sem=out,
                    recv_sem=into,
                    device_id=sibling,
                    device_id_type=MESH,
                ).start()
        live["core", u] = pltpu.make_async_remote_copy(
            src_ref=buf["got", u],
            dst_ref=buf["got", u],
            send_sem=out,
            recv_sem=into,
            device_id=sibling,
            device_id_type=MESH,
        )
        pending.append(("core", u))

    def add_rows(dst, src, rows):
        @pl.loop(0, rows // 32)
        def _(i):
            at = pl.ds(pl.multiple_of(i * 32, 32), 32)
            dst[at, :] = dst[at, :] + src[at, :]

    def add_blocks(own, got, xl_at):
        @pl.loop(0, 4 * ROWS // 32)
        def _(i):
            b, at = lax.div(i, 4), pl.ds(pl.multiple_of(lax.rem(i, 4) * 32, 32), 32)
            own[xl_at, b, at, :] = own[xl_at, b, at, :] + got[xl_at, b, at, :]

    def mix(u):
        loaded(("own", u))
        arrive(("core", u))
        own, got = buf["own", u], buf["got", u]
        add_blocks(own, got, 1 - xl)
        add_blocks(own, got, xl)

    def send_pair(u):
        send(("px", u), buf["own", u].at[1 - xl], buf["px", u], pair)

    def cross(u):
        arrive(("px", u))
        own, px = buf["own", u], buf["px", u]

        @pl.loop(0, 4 * ROWS // 32)
        def _(i):
            b, at = lax.div(i, 4), pl.ds(pl.multiple_of(lax.rem(i, 4) * 32, 32), 32)
            own[xl, b, at, :] = own[xl, b, at, :] + px[b, at, :]

    half = ROWS // 2
    low, high = pl.ds(0, half), pl.ds(half, half)

    def block(u, at, rows):
        own = buf["own", u]
        return own.at[xl, at, rows] if UNITS[u][0] == "x" else own.at[:, at, rows]

    def first(u):
        send(("t1p", u), block(u, other(2), low), buf["t1p", u], near("y", 1))
        send(("t1m", u), block(u, other(2), high), buf["t1m", u], near("y", -1))
        send(("f1p", u), block(u, other(1), high), buf["f1p", u], near("y", 1))
        send(("f1m", u), block(u, other(-1), low), buf["f1m", u], near("y", -1))

    def add_into(u, at, start, src):
        own = buf["own", u]
        if UNITS[u][0] == "x":
            add_rows(own.at[xl, at, pl.ds(start, half)], src, half)
        else:
            for i in range(2):
                add_rows(own.at[i, at, pl.ds(start, half)], src.at[i], half)

    def second(u):
        arrive(("t1p", u))
        add_into(u, other(1), 0, buf["t1p", u])
        send(("f2p", u), block(u, other(1), low), buf["f2p", u], near("y", 1))
        arrive(("t1m", u))
        add_into(u, other(-1), half, buf["t1m", u])
        send(("f2m", u), block(u, other(-1), high), buf["f2m", u], near("y", -1))

    def update(u, h, t, summed):
        at = pl.ds(pl.multiple_of(h * half + t * 16, 16), 16)
        new = inner_step(summed, buf["first", u][at, :], buf["second", u][at, :])
        sent = buf["sent", u]
        for fam, _, w, start in part_starts(u):
            cols = pl.ds(start, w)
            piece = new[:, start : start + w]
            if fam == "p":
                sent[lax.div(t, 2), 2 * lax.rem(t, 2), h * 8 : h * 8 + 8, cols] = piece[:8].astype(BF)
                sent[lax.div(t, 2), 2 * lax.rem(t, 2) + 1, h * 8 : h * 8 + 8, cols] = piece[8:].astype(BF)
            else:
                sent[h, t, :, cols] = piece.astype(BF)

    def states_ready(u):
        for name in ("first", "second"):
            loaded((name, u))

    def third(u):
        for name in ("f1p", "f1m", "f2p", "f2m"):
            arrive((name, u))
        own = buf["own", u]
        if UNITS[u][0] == "x":
            states_ready(u)
        for h, (one, two) in enumerate((("f2p", "f1m"), ("f1p", "f2m"))):
            if UNITS[u][0] == "x":

                @pl.loop(0, 4)
                def _(t, h=h, one=one, two=two):
                    at = pl.ds(pl.multiple_of(t * 16, 16), 16)
                    mine = own[xl, y, pl.ds(pl.multiple_of(h * half + t * 16, 16), 16), :].astype(F32)
                    total = mine + buf[one, u][at, :].astype(F32) + buf[two, u][at, :].astype(F32)
                    update(u, h, t, total)
            else:

                @pl.loop(0, 8)
                def _(i, h=h, one=one, two=two):
                    b, t = lax.div(i, 4), lax.rem(i, 4)
                    at = pl.ds(pl.multiple_of(t * 16, 16), 16)
                    to = pl.ds(pl.multiple_of(h * half + t * 16, 16), 16)
                    total = own[b, y, to, :].astype(F32) + buf[one, u][b, at, :].astype(F32)
                    own[b, y, to, :] = (total + buf[two, u][b, at, :].astype(F32)).astype(BF)
        if UNITS[u][0] == "x":
            spread(u)

    def back(u):
        send(("bx", u), buf["own", u].at[1 - xl, y], buf["bx", u], pair)

    def final(u):
        arrive(("bx", u))
        states_ready(u)
        own, bx = buf["own", u], buf["bx", u]
        for h in range(2):

            @pl.loop(0, 4)
            def _(t, h=h):
                at = pl.ds(pl.multiple_of(h * half + t * 16, 16), 16)
                update(u, h, t, own[xl, y, at, :].astype(F32) + bx[at, :].astype(F32))

        spread(u)

    def spread(u):
        for by in (1, 2, 3):
            send(("repl", u, by), buf["sent", u].at[:, lax.rem(z + by, 4)], buf["repl", u].at[by - 1], near("z", by))

    def repl(u):
        for by in (1, 2, 3):
            arrive(("repl", u, by))
        sent, got, part = buf["sent", u], buf["repl", u], buf["part", u]
        for b in (1 - xh, xh):
            total = sent[b, z].astype(F32) + got[0, b].astype(F32) + got[1, b].astype(F32) + got[2, b].astype(F32)
            part[b] = total.astype(BF)
        send(("far", u), part.at[1 - xh], buf["far", u], opposite)

    def far(u):
        arrive(("far", u))
        for fam, off, w, at in part_starts(u):
            cols, to = pl.ds(at, w), pl.ds(natural(fam, off), w)
            steps = buf["part", u][xh, :, cols].astype(F32) + buf["far", u][:, cols].astype(F32)
            anchor = buf["anchor"][:, to]
            pseudo = anchor - (buf["all"][:, to] - steps / 8.0)
            velocity_next = momentum_keep * buf["velocity"][:, to] + pseudo
            anchor_next = anchor - outer_rate * (pseudo + momentum_keep * velocity_next)
            outer[0, :, to] = anchor_next
            outer[1, :, to] = velocity_next
            buf["fresh", UNITS[u][1]][:, pl.ds(unit_start(u) + at, w)] = anchor_next.astype(BF)

    def slot(dim, by=0):
        at = lax.rem(here[dim] + by + 4, 4)
        return lax.rem(at, 2) * 2 + lax.div(at, 2) if dim == "x" else at

    def gather(stage, g):
        k, at, w, (d1, d2, d3) = GATHER_LIST[g]
        whole = full[g]
        if stage == 0:
            mine = whole.at[c, slot(d3), slot(d2), slot(d1)]
            mine[...] = buf["fresh", k][:, pl.ds(at, w)]
            for by in (2, 1, 3):
                send(("g", g, "0", by), mine, mine, near(d1, by))
        elif stage == 1:
            for by in (1, 3, 2):
                arrive(("g", g, "0", by))
            mine = whole.at[c, slot(d3), slot(d2)]
            for by in (2, 1, 3):
                send(("g", g, "1", by), mine, mine, near(d2, by))
        elif stage == 2:
            for by in (1, 3, 2):
                arrive(("g", g, "1", by))
            for turn in (0, 1):
                for by, part in ((1, 0), (3, 2)):
                    some = whole.at[c, slot(d3), pl.ds(part if turn == 0 else 2 - part, 2)]
                    send(("g", g, "2", by, turn), some, some, near(d3, by))
        elif stage == 3:
            for by, part in ((1, 0), (3, 2)):
                arrive(("g", g, "2", by, 0))
                some = whole.at[c, slot(d3, -by), pl.ds(part, 2)]
                send(("g", g, "3", by), some, some, near(d3, by))
        elif stage == 4:
            mine = whole.at[c, slot(d3)]
            send(("g", g, "s", 0), mine, mine, sibling)
            for by in (1, 3):
                arrive(("g", g, "2", by, 1))
                got = whole.at[c, slot(d3, -by)]
                send(("g", g, "s", by), got, got, sibling)
        elif stage == 5:
            for by, part in ((1, 0), (3, 2)):
                arrive(("g", g, "3", by))
                some = whole.at[c, slot(d3, 2), pl.ds(part, 2)]
                send(("g", g, "t", by), some, some, sibling)
        else:
            for key in (("s", 0), ("s", 1), ("s", 3), ("t", 1), ("t", 3)):
                arrive(("g", g) + key)

    def drain():
        for key in list(pending):
            arrive(key)
        for key in list(unread):
            loaded(key)
        for copy in live.values():
            copy.wait_send()

    acts = {
        GREET: greet, MEET: meet, CORE: core, LOAD: load, ROWS_IN: load_rows, BASE: base_send, STATES: load_states,
        MIX: mix, PX: send_pair, FIRST: first, SECOND: second, CROSS: cross, THIRD: third, BACK: back, FINAL: final,
        SUM: base_sum, REPL: repl, FAR: far, ALL: base_all, GATHER: gather, DRAIN: drain,
    }
    for act, *where in SCHEDULE:
        acts[act](*where)


def gather_shape(g):
    _, _, w, _ = GATHER_LIST[g]
    return (2, 4, 4, 4, 16, w)


def run_step(args):
    s = make_scratch()
    outs = [pltpu.VMEM(gather_shape(g), BF) for g in range(len(GATHER_LIST))]
    outs.append(pltpu.VMEM((2, 16, TOTAL), F32))

    def kernel(*refs):
        step_kernel(s.names, *refs)

    return pl.pallas_call(
        kernel,
        out_shape=outs,
        in_specs=[pl.BlockSpec(memory_space=pltpu.HBM)] * 12,
        out_specs=[pl.BlockSpec(memory_space=pltpu.VMEM)] * len(outs),
        scratch_shapes=s.shapes + [pltpu.SemaphoreType.DMA((N_SEM,))],
        compiler_params=pltpu.CompilerParams(
            collective_id=0, has_side_effects=True, vmem_limit_bytes=48 * 2**20
        ),
        name="outer_step",
    )(*args)


def column_pieces():
    out = []
    for g, (k, at, w, _) in enumerate(GATHER_LIST):
        for u in range(len(UNITS)):
            if UNITS[u][1] != k:
                continue
            for fam, off, wide, start in part_starts(u):
                begin = unit_start(u) + start
                lo, hi = max(begin, at), min(begin + wide, at + w)
                if lo < hi:
                    out.append((g, lo - at, hi - lo, fam, off + lo - begin))
    return out


def place_kernel(*refs):
    n = len(GATHER_LIST)
    full, outer = refs[:n], refs[n]
    weights_pair, weights_down, anchor_pair, anchor_down, velocity_pair, velocity_down = refs[n + 1 : n + 7]
    pair_rows, down_rows, sems = refs[n + 7 :]

    for i, (pair, down) in enumerate(((anchor_pair, anchor_down), (velocity_pair, velocity_down))):
        pair[0] = outer[i, :8, : WIDE["p"]]
        pair[1] = outer[i, 8:, : WIDE["p"]]
        down[...] = outer[i, :, WIDE["p"] :]

    @pl.loop(0, 16)
    def _(q):
        c, y, xl = lax.rem(q, 2), lax.rem(lax.div(q, 2), 4), lax.div(q, 8)

        def block(g, r):
            index = {"x": xl * 2 + r // 4, "y": y, "z": r % 4}
            return (c,) + tuple(index[d] for d in reversed(GATHER_LIST[g][3]))

        start = {fam: pl.multiple_of(q * WIDE[fam], 128) for fam in WIDE}
        for g, at, w, fam, col in column_pieces():
            to = pl.ds(pl.multiple_of(start[fam] + col, 128), w)
            for m in range(4):
                one = full[g][block(g, 2 * m) + (slice(None), slice(at, at + w))]
                two = full[g][block(g, 2 * m + 1) + (slice(None), slice(at, at + w))]
                if fam == "d":
                    down_rows[32 * m : 32 * m + 16, to] = one
                    down_rows[32 * m + 16 : 32 * m + 32, to] = two
                else:
                    for half in range(2):
                        rows = slice(8 * half, 8 * half + 8)
                        pair_rows[half, 16 * m : 16 * m + 16, to] = jnp.concatenate([one[rows], two[rows]], axis=0)
        cols = pl.ds(start["p"], WIDE["p"])
        pltpu.make_async_copy(pair_rows.at[:, :, cols], weights_pair.at[:, :, cols], sems.at[0]).start()
        cols = pl.ds(start["d"], WIDE["d"])
        pltpu.make_async_copy(down_rows.at[:, cols], weights_down.at[:, cols], sems.at[1]).start()

    pltpu.make_async_copy(pair_rows, weights_pair, sems.at[0]).wait()
    pltpu.make_async_copy(down_rows, weights_down, sems.at[1]).wait()


def run_place(full, outer):
    vmem = pl.BlockSpec(memory_space=pltpu.VMEM)
    hbm = pl.BlockSpec(memory_space=pltpu.HBM)
    return pl.pallas_call(
        place_kernel,
        out_shape=[
            jax.ShapeDtypeStruct((2, 64, 28672), BF),
            jax.ShapeDtypeStruct((128, 8192), BF),
            jax.ShapeDtypeStruct((2, 8, 1792), F32),
            jax.ShapeDtypeStruct((16, 512), F32),
            jax.ShapeDtypeStruct((2, 8, 1792), F32),
            jax.ShapeDtypeStruct((16, 512), F32),
        ],
        in_specs=[vmem] * (len(full) + 1),
        out_specs=[hbm, hbm, vmem, vmem, vmem, vmem],
        scratch_shapes=[
            pltpu.VMEM((2, 64, 28672), BF),
            pltpu.VMEM((128, 8192), BF),
            pltpu.SemaphoreType.DMA((2,)),
        ],
        compiler_params=pltpu.CompilerParams(vmem_limit_bytes=32 * 2**20),
        name="place",
    )(*full, outer)


def body(
    grads_pair,
    grads_down,
    inner_pair,
    inner_down,
    first_pair,
    first_down,
    second_pair,
    second_down,
    anchor_pair,
    anchor_down,
    velocity_pair,
    velocity_down,
):
    args = [
        grads_pair.reshape(128, 28672),
        grads_down.reshape(128, 8192),
        inner_pair.reshape(128, 1792),
        inner_down.reshape(128, 512),
        first_pair.reshape(128, 1792),
        first_down.reshape(128, 512),
        second_pair.reshape(128, 1792),
        second_down.reshape(128, 512),
        anchor_pair.reshape(128, 1792),
        anchor_down,
        velocity_pair.reshape(128, 1792),
        velocity_down,
    ]
    *full, outer = run_step(args)
    return tuple(run_place(full, outer))


def solution(mesh):
    in_specs = (
        P(("replica", "zero"), None, None, None),
        P(("replica", "zero"), None, None),
        P("replica", None, None, "zero"),
        P("replica", None, "zero"),
        P("replica", None, None, "zero"),
        P("replica", None, "zero"),
        P("replica", None, None, "zero"),
        P("replica", None, "zero"),
        P(None, None, "zero"),
        P(None, "zero"),
        P(None, None, "zero"),
        P(None, "zero"),
    )
    out_specs = (
        P(),
        P(),
        P(None, "replica", "zero"),
        P("replica", "zero"),
        P(None, "replica", "zero"),
        P("replica", "zero"),
    )
    return jax.shard_map(body, mesh=mesh, in_specs=in_specs, out_specs=out_specs, check_vma=False)
```
